128 devices in a mesh: seq: 32 (over z, x, core), wsh: 4 (over y).
Axes of the slice: x: 4, y: 4, z: 4, core: 2. Of those that a mesh axis runs over, the one named last changes fastest.
Arguments:
- inputs: bfloat16 [8, 4096, 1024], P('wsh', 'seq'), may hold values from -6 to 6
- lengths: int32 [8], P('wsh'), may hold values from 1024 to 4096, as said below
- norm_gain: bfloat16 [1024], P('wsh'), may hold values from 0.5 to 1.5
- w_query: bfloat16 [1024, 512], P('wsh'), may hold values from -0.1875 to 0.1875
- w_key: bfloat16 [1024, 512], P('wsh'), may hold values from -0.1875 to 0.1875
- w_value: bfloat16 [1024, 1024], P('wsh'), may hold values from -0.1875 to 0.1875
- w_outgate: bfloat16 [1024, 1024], P('wsh'), may hold values from -0.1875 to 0.1875
- w_rank_in: bfloat16 [1024, 16], P('wsh'), may hold values from -0.1875 to 0.1875
- w_rank_out: bfloat16 [16, 512], P('wsh'), may hold values from -1.5 to 1.5
- rank_bias: bfloat16 [512], P('wsh'), may hold values from -1 to 8
- head_gain: bfloat16 [256], P('wsh'), may hold values from 0.099609375 to 1.8984375
- w_output: bfloat16 [1024, 1024], P('wsh'), may hold values from -0.25 to 0.25
- ffn_gain: bfloat16 [1024], P('wsh'), may hold values from 0.5 to 1.5
- w_gate: bfloat16 [1024, 2816], P('wsh'), may hold values from -0.1875 to 0.1875
- w_up: bfloat16 [1024, 2816], P('wsh'), may hold values from -0.1875 to 0.1875
- w_down: bfloat16 [2816, 1024], P('wsh'), may hold values from -0.21875 to 0.21875
- cotangent: bfloat16 [8, 4096, 1024], P('wsh', 'seq'), may hold values from -6 to 6
Outputs:
- outputs: float32 [8, 4096, 1024], P('wsh', 'seq')
- input_grad: float32 [8, 4096, 1024], P('wsh', 'seq')
- grad_norm_gain: float32 [1024], P('wsh')
- grad_query: float32 [1024, 512], P('wsh')
- grad_key: float32 [1024, 512], P('wsh')
- grad_value: float32 [1024, 1024], P('wsh')
- grad_outgate: float32 [1024, 1024], P('wsh')
- grad_rank_in: float32 [1024, 16], P('wsh')
- grad_rank_out: float32 [16, 512], P('wsh')
- grad_rank_bias: float32 [512], P('wsh')
- grad_head_gain: float32 [256], P('wsh')
- grad_output: float32 [1024, 1024], P('wsh')
- grad_ffn_gain: float32 [1024], P('wsh')
- grad_gate: float32 [1024, 2816], P('wsh')
- grad_up: float32 [1024, 2816], P('wsh')
- grad_down: float32 [2816, 1024], P('wsh')
The draws below stay inside these ranges and needn't reach their ends.
Inputs may be any that keep to these rules, and one draw needn't show every extreme that they name: `lengths`: of the 2 sequences on each index of wsh, one (chosen at random) has the full length 4096.
All inputs are finite; a program needn't handle non-finite values.
Results may differ from the reference program's by a relative error of at most 0.029.
Values may be sent and summed in bfloat16 or wider, within the bound.
No kernel may reach another device: no remote copies, remote signals or barrier semaphores. Data moves between devices by JAX's collectives and lax.ppermute only.
A program may use at most 320 MiB of HBM per device.

```python
import jax
import jax.numpy as jnp
from jax import lax

D = 1024
H = 4
HK = 128
HV = 256
R = 16
FF = 2816
CH = 64
SEQS = 2
K = 512
V = 1024
SLOT = 4096
BATCH = 8


def draw_lengths(key, part):
    key = jax.random.fold_in(key, 11)
    key_ragged, key_full = jax.random.split(key)
    groups = BATCH // SEQS
    ragged = jax.random.randint(key_ragged, (groups, SEQS), SLOT // 4, SLOT + 1)
    chosen = jax.random.randint(key_full, (groups, 1), 0, SEQS)
    picked = jnp.arange(SEQS)[None, :] == chosen
    return jnp.where(picked, SLOT, ragged).reshape(BATCH).astype(jnp.int32)


def block_scale(own_key, extent, cuts, low, largest):
    factor_of = 1.0
    for position, parts in cuts:
        draws = jax.random.uniform(jax.random.fold_in(jax.random.fold_in(own_key, 6), position), (parts,), jnp.float32, low / len(cuts), largest / len(cuts))
        factor_of = factor_of * jnp.repeat(jnp.exp(draws), extent[position] // parts).reshape((-1,) + (1,) * (len(extent) - 1 - position))
    return factor_of


def noise(key, dims, spread, reach, cuts=(), kind=jnp.bfloat16):
    array = spread * jax.random.normal(key, dims, jnp.float32)
    if cuts:
        array = array * block_scale(key, dims, cuts, -0.22, 0.18)
    return jnp.clip(array, -reach, reach).astype(kind)


def setup_inputs(seed: int = 0) -> dict:
    streams_of = jax.random.split(jax.random.key(seed), 18)
    inputs = noise(streams_of[0], (BATCH, SLOT, D), 1.0, 6.0, ((0, 4), (1, 32)))
    lengths = draw_lengths(jax.random.fold_in(streams_of[17], 71), 0)
    norm_gain = jnp.clip(1.0 + 0.1 * jax.random.normal(streams_of[2], (D,), jnp.float32), 0.5, 1.5).astype(jnp.bfloat16)
    w_query = noise(streams_of[3], (D, K), D ** -0.5, 0.1875, ((0, 4),))
    w_key = noise(streams_of[4], (D, K), D ** -0.5, 0.1875, ((0, 4),))
    w_value = noise(streams_of[5], (D, V), D ** -0.5, 0.1875, ((0, 4),))
    w_outgate = noise(streams_of[6], (D, V), D ** -0.5, 0.1875, ((0, 4),))
    w_rank_in = noise(streams_of[7], (D, R), D ** -0.5, 0.1875, ((0, 4),))
    w_rank_out = noise(streams_of[8], (R, K), R ** -0.5, 1.5, ((0, 4),))
    rank_bias = jnp.clip(-1.0 + 9.0 * jax.random.uniform(streams_of[9], (K,), jnp.float32) ** block_scale(streams_of[9], (K,), ((0, 4),), -0.2, 0.2), -1.0, 8.0).astype(jnp.bfloat16)
    head_gain = jnp.clip(1.0 + 0.18 * jax.random.normal(streams_of[10], (HV,), jnp.float32), 0.099609375, 1.8984375).astype(jnp.bfloat16)
    w_output = noise(streams_of[11], (V, D), (V // 2) ** -0.5, 0.25, ((0, 4),))
    ffn_gain = jnp.clip(1.0 + 0.1 * jax.random.normal(streams_of[12], (D,), jnp.float32), 0.5, 1.5).astype(jnp.bfloat16)
    w_gate = noise(streams_of[13], (D, FF), D ** -0.5, 0.1875, ((0, 4),))
    w_up = noise(streams_of[14], (D, FF), D ** -0.5, 0.1875, ((0, 4),))
    w_down = noise(streams_of[15], (FF, D), (FF // 4) ** -0.5, 0.21875, ((0, 4),))
    cotangent = noise(streams_of[16], (BATCH, SLOT, D), 1.0, 6.0, ((0, 4), (1, 32)))
    return {"inputs": inputs, "lengths": lengths, "norm_gain": norm_gain, "w_query": w_query, "w_key": w_key, "w_value": w_value, "w_outgate": w_outgate, "w_rank_in": w_rank_in, "w_rank_out": w_rank_out, "rank_bias": rank_bias, "head_gain": head_gain, "w_output": w_output, "ffn_gain": ffn_gain, "w_gate": w_gate, "w_up": w_up, "w_down": w_down, "cotangent": cotangent}


EPS = 1e-06
DECAY_NORM = 16.0
PRECISION_LEVEL = lax.Precision.HIGHEST

@jax.custom_vjp
def low(v):
    return lax.optimization_barrier(v.astype(jnp.bfloat16)).astype(jnp.float32)

@jax.custom_vjp
def low_back(v):
    return v

def low_keep(v):
    return (low(v), None)

def low_pass(kept, grad):
    return (grad,)

def back_keep(v):
    return (v, None)

def back_low(kept, grad):
    return (low(grad),)
low.defvjp(low_keep, low_pass)
low_back.defvjp(back_keep, back_low)

def matmul(left, right):
    return jnp.dot(left, right, precision=PRECISION_LEVEL, preferred_element_type=jnp.float32)

def rms_scale(values):
    return values * lax.rsqrt(lax.optimization_barrier(jnp.mean(values * values, axis=-1, keepdims=True)) + EPS)

def block_step(incoming_state, block_item):
    queries, key_rows, value_matrix_rows, decays = block_item
    within = jnp.cumsum(decays, axis=0)
    final_decay_sum = within[-1]
    query_decayed = queries * jnp.exp(within)
    k_dec = key_rows * jnp.exp(-within)
    key_final_decay = key_rows * jnp.exp(final_decay_sum[None] - within)
    block_len = queries.shape[0]
    causal = jnp.tril(jnp.ones((block_len, block_len), jnp.float32))
    scores = jnp.einsum('thk,uhk->htu', query_decayed, k_dec, precision=PRECISION_LEVEL) * causal[None]
    mixer_output_rows = jnp.einsum('htu,uhv->thv', scores, value_matrix_rows, precision=PRECISION_LEVEL)
    mixer_output_rows = mixer_output_rows + jnp.einsum('cnd,ndr->cnr', query_decayed, incoming_state, precision=PRECISION_LEVEL)
    updated_state = jnp.exp(final_decay_sum)[:, :, None] * incoming_state + jnp.einsum('qij,qip->ijp', key_final_decay, value_matrix_rows, precision=PRECISION_LEVEL)
    return (updated_state, mixer_output_rows)

def mixer(queries, key_rows, value_matrix_rows, decays):
    blocks = SLOT // CH

    def blocked(values):
        return values.reshape(blocks, CH, H, values.shape[-1])
    initial = jnp.zeros((H, HK, HV), jnp.float32)
    carried, pieces = lax.scan(jax.checkpoint(block_step), initial, (blocked(queries), blocked(key_rows), blocked(value_matrix_rows), blocked(decays)))
    return pieces.reshape(SLOT, H, HV)

def layer(inputs, weights):
    norm_gain, w_query, w_key, w_value, w_outgate, w_rank_in, w_rank_out, rank_bias, head_gain, w_output, ffn_gain, w_gate, w_up, w_down = weights
    normed = low(rms_scale(inputs) * norm_gain)
    queries = low_back(low(matmul(normed, w_query))) * HK ** (-0.5)
    key_rows = low_back(low(matmul(normed, w_key)))
    value_matrix_rows = low_back(low(matmul(normed, w_value)))
    outgate = low_back(matmul(normed, w_outgate))
    rank_rows = low_back(low(matmul(normed, w_rank_in)))
    logits = low_back(matmul(rank_rows, w_rank_out) + rank_bias)
    decays = jax.nn.log_sigmoid(logits) / DECAY_NORM
    mixed = mixer(queries.reshape(SLOT, H, HK), key_rows.reshape(SLOT, H, HK), value_matrix_rows.reshape(SLOT, H, HV), decays.reshape(SLOT, H, HK))
    gate_heads = outgate.reshape(SLOT, H, HV)
    branch = rms_scale(mixed) * head_gain * (gate_heads * jax.nn.sigmoid(gate_heads))
    branch = low_back(low(branch.reshape(SLOT, V)))
    middle = inputs + low_back(matmul(branch, w_output))
    second = low(rms_scale(middle) * ffn_gain)
    gate_rows = low_back(matmul(second, w_gate))
    up_rows = low_back(matmul(second, w_up))
    hidden = low_back(low(jax.nn.silu(gate_rows) * up_rows))
    return middle + matmul(hidden, w_down)

def reference(inputs, lengths, norm_gain, w_query, w_key, w_value, w_outgate, w_rank_in, w_rank_out, rank_bias, head_gain, w_output, ffn_gain, w_gate, w_up, w_down, cotangent):
    weights = tuple((weight.astype(jnp.float32) for weight in (norm_gain, w_query, w_key, w_value, w_outgate, w_rank_in, w_rank_out, rank_bias, head_gain, w_output, ffn_gain, w_gate, w_up, w_down)))
    positions = jnp.arange(SLOT, dtype=jnp.int32)

    def add_pair(total, grad):
        return total + grad

    def one_sequence(totals, seq_item):
        seq_rows, seq_length, grad_rows = seq_item
        valid = (positions < seq_length).astype(jnp.float32)[:, None]
        result, pull = jax.vjp(layer, seq_rows.astype(jnp.float32), weights)
        grad_in, grad_weights = pull(grad_rows.astype(jnp.float32) * valid)
        totals = jax.tree.map(add_pair, totals, grad_weights)
        return (totals, (result, grad_in))
    zeros = tuple((jnp.zeros_like(weight) for weight in weights))
    totals, (outputs, input_grad) = lax.scan(one_sequence, zeros, (inputs, lengths, cotangent))
    return (outputs, input_grad, totals[0], totals[1], totals[2], totals[3], totals[4], totals[5], totals[6], totals[7], totals[8], totals[9], totals[10], totals[11], totals[12], totals[13])
```

```python
import functools

import jax
import jax.numpy as jnp
from jax import lax
from jax.experimental import pallas as pl
from jax.experimental.pallas import tpu as pltpu
from jax.sharding import PartitionSpec as P

H = 4
HK = 128
HV = 256
EPS = 1e-06
DECAY_NORM = 16.0
QS = HK ** (-0.5)
BF = jnp.bfloat16
F32 = jnp.float32
HIGH = lax.Precision.HIGHEST
FFP = 768
VMEM = 50 * 1024 * 1024


def params():
    return pltpu.CompilerParams(
        dimension_semantics=("arbitrary",), vmem_limit_bytes=VMEM
    )


def moved(index, axis, by):
    if axis == "y":
        return (index + by) % 4
    core, x, z = index % 2, (index // 2) % 4, index // 8
    if axis == "c":
        core = 1 - core
    elif axis == "x":
        x = (x + by) % 4
    else:
        z = (z + by) % 4
    return (z * 4 + x) * 2 + core


def shift(value, axis, by=1):
    name, count = ("wsh", 4) if axis == "y" else ("seq", 32)
    return lax.ppermute(value, name, [(i, moved(i, axis, by)) for i in range(count)])


def fetch(value, axis):
    far = {d: shift(value, axis, -d) for d in (2, 1, 3)}
    return [value, far[1], far[2], far[3]]


def spread(block, axis):
    far = {d: shift(block(d), axis, d) for d in (2, 1, 3)}
    total = block(0).astype(F32)
    for d in (1, 2, 3):
        total = total + far[d].astype(F32)
    return total


def pick(value, index, axis=0):
    return lax.dynamic_index_in_dim(value, index, axis, keepdims=False)


def in_order(pieces, me):
    rows = pieces[0].shape[0]
    both = jnp.concatenate(pieces + pieces[:3], axis=0)
    return lax.dynamic_slice_in_dim(both, ((4 - me) % 4) * rows, 4 * rows, axis=0)


def from_me(value, me):
    both = jnp.concatenate([value, value[:3]], axis=0)
    return lax.dynamic_slice_in_dim(both, me, 4, axis=0)


def after(value, *others):
    return lax.optimization_barrier((value,) + others)[0]


def dot_nn(a, b, precision=None):
    return lax.dot_general(
        a, b, (((1,), (0,)), ((), ())), precision=precision, preferred_element_type=F32
    )


def dot_nt(a, b, precision=None):
    return lax.dot_general(
        a, b, (((1,), (1,)), ((), ())), precision=precision, preferred_element_type=F32
    )


def dot_tn(a, b, precision=None):
    return lax.dot_general(
        a, b, (((0,), (0,)), ((), ())), precision=precision, preferred_element_type=F32
    )


def causal_mask():
    rows = lax.broadcasted_iota(jnp.int32, (128, 128), 0)
    cols = lax.broadcasted_iota(jnp.int32, (128, 128), 1)
    return rows >= cols


def log_row(total):
    high = total.astype(BF)
    low = (total - high.astype(F32)).astype(BF)
    return jnp.concatenate([high, low], axis=1)


def read_logs(ref):
    tail = ref[512:528, :].astype(F32)
    return tail[:, :128] + tail[:, 128:]


def proj_kernel(sc, x, gain, wro, bias, *refs):
    pieces, outs = refs[:21], refs[21:]
    normed, wqr, wog, qkv, og, rank, logits, within, oi, spk = outs
    h = pl.program_id(0)
    y, c = sc[0], sc[1]

    def halves(part):
        for d in (1, 2, 3):
            for who, half in ((0, c), (1, 1 - c)):
                yield 256 * d + 128 * half, pieces[3 + 6 * (d - 1) + 3 * who + part]

    @pl.when(h == 0)
    def _():
        xf = x[...].astype(F32)
        scale = lax.rsqrt(jnp.mean(xf * xf, axis=-1, keepdims=True) + EPS)
        for j in range(4):
            at = pl.multiple_of(((y + j) % 4) * 256, 256)
            part = x[:, pl.ds(at, 256)].astype(F32) * scale
            normed[:, j * 256 : j * 256 + 256] = (
                part * gain[:, j * 256 : j * 256 + 256]
            ).astype(BF)
        wqr[0:256, 2048:2176] = pieces[2][...]
        for at, ref in halves(2):
            wqr[pl.ds(pl.multiple_of(at, 128), 128), 2048:2176] = ref[...]
        rank[...] = dot_nn(normed[...], wqr[:, 2048:2176]).astype(BF)
        spk[:, 512:528, :] = jnp.zeros((2, 16, 256), BF)

    left = pl.multiple_of(h * 512, 512)
    wqr[0:256, pl.ds(left, 512)] = pieces[0][...]
    for at, ref in halves(0):
        wqr[pl.ds(pl.multiple_of(at, 128), 128), pl.ds(left, 512)] = ref[...]
    wog[0:256, :] = pieces[1][...]
    for at, ref in halves(1):
        wog[pl.ds(pl.multiple_of(at, 128), 128), :] = ref[...]
    nb = normed[...]
    rows = dot_nn(nb, wqr[:, pl.ds(left, 512)]).astype(BF)
    qkv[...] = rows
    og[...] = dot_nn(nb, wog[...])
    lg = dot_nn(rank[...], wro[...]) + bias[...]
    logits[...] = lg
    decays = (jnp.minimum(lg, 0.0) - jnp.log1p(jnp.exp(-jnp.abs(lg)))) / DECAY_NORM
    mask = causal_mask()
    tri = mask.astype(F32)
    for b in range(2):
        r = slice(128 * b, 128 * b + 128)
        w = dot_nn(tri, decays[r], HIGH)
        within[r, :] = w
        q = rows[r, 0:128].astype(F32) * QS
        k = rows[r, 128:256].astype(F32)
        v = rows[r, 256:512]
        mid, tot = w[63:64], w[127:128]
        qm = (q * jnp.exp(w - mid)).astype(BF)
        km = (k * jnp.exp(mid - w)).astype(BF)
        scores = jnp.where(mask, dot_nt(qm, km), 0.0).astype(BF)
        oi[r, :] = dot_nn(scores, v)
        kend = (k * jnp.exp(tot - w)).astype(BF)
        spk[b, pl.ds(pl.multiple_of(h * 128, 128), 128), :] = dot_tn(kend, v).astype(BF)
        line = lax.broadcasted_iota(jnp.int32, (16, 256), 0)
        row = jnp.broadcast_to(log_row(tot).astype(F32), (16, 256))
        old = spk[b, 512:528, :].astype(F32)
        spk[b, 512:528, :] = jnp.where(line == h, row, old).astype(BF)


def project_rows(sc, x, gain, wro, bias, own, mine, got):
    def cols(rows, width, at):
        return pl.BlockSpec((rows, width), lambda h, s, at=at: (0, at(h)))

    def three(rows):
        return [
            cols(rows, 512, lambda h: h),
            cols(rows, 256, lambda h: 8 + h),
            cols(rows, 128, lambda h: 24),
        ]

    def whole(shape):
        return pl.BlockSpec(shape, lambda h, s: (0,) * len(shape))

    arrays, specs = [own] * 3, three(256)
    for m, g in zip(mine, got):
        arrays += [m] * 3 + [g] * 3
        specs += three(128) * 2
    out = lambda shape, dtype: jax.ShapeDtypeStruct(shape, dtype)
    return pl.pallas_call(
        proj_kernel,
        grid_spec=pltpu.PrefetchScalarGridSpec(
            num_scalar_prefetch=1,
            grid=(4,),
            in_specs=[
                whole((256, 1024)),
                whole((1, 1024)),
                cols(128, 128, lambda h: h),
                cols(1, 128, lambda h: h),
            ]
            + specs,
            out_specs=[
                whole((256, 1024)),
                whole((1024, 2176)),
                cols(1024, 256, lambda h: h),
                cols(256, 512, lambda h: h),
                cols(256, 256, lambda h: h),
                whole((256, 128)),
                cols(256, 128, lambda h: h),
                cols(256, 128, lambda h: h),
                cols(256, 256, lambda h: h),
                whole((2, 528, 256)),
            ],
        ),
        out_shape=[
            out((256, 1024), BF),
            out((1024, 2176), BF),
            out((1024, 1024), BF),
            out((256, 2048), BF),
            out((256, 1024), F32),
            out((256, 128), BF),
            out((256, 512), F32),
            out((256, 512), F32),
            out((256, 1024), F32),
            out((2, 528, 256), BF),
        ],
        compiler_params=params(),
        cost_estimate=pl.CostEstimate(
            flops=2 * 256 * 1024 * 3200, bytes_accessed=20_000_000, transcendentals=600_000
        ),
        name="project_rows",
    )(sc, x, gain, wro, bias, *arrays)


def core_kernel(sc, mine, got, chip):
    front = sc[0] == 0
    first_logs = jnp.where(front, read_logs(mine), read_logs(got))
    second_logs = jnp.where(front, read_logs(got), read_logs(mine))
    factor = jnp.transpose(jnp.exp(second_logs))
    for h in range(4):
        r = slice(128 * h, 128 * h + 128)
        a, b = mine[r, :].astype(F32), got[r, :].astype(F32)
        f = factor[:, h : h + 1]
        chip[r, :] = (jnp.where(front, a, b) * f + jnp.where(front, b, a)).astype(BF)
    chip[512:528, :] = log_row(first_logs + second_logs)


def axis_kernel(sc, p0, p1, p2, p3, total, before):
    pos = sc[0]
    pieces = (p0, p1, p2, p3)
    places = [(pos - d + 4) % 4 for d in range(4)]
    logs = [read_logs(p) for p in pieces]
    all_f, before_f = [], []
    for place in places:
        late = jnp.zeros_like(logs[0])
        late_here = jnp.zeros_like(logs[0])
        for other, log in zip(places, logs):
            late = late + jnp.where(other > place, log, 0.0)
            late_here = late_here + jnp.where((other > place) & (other < pos), log, 0.0)
        all_f.append(jnp.transpose(jnp.exp(late)))
        before_f.append(jnp.transpose(jnp.where(place < pos, jnp.exp(late_here), 0.0)))
    for h in range(4):
        r = slice(128 * h, 128 * h + 128)
        states = [p[r, :].astype(F32) for p in pieces]
        total[r, :] = sum(f[:, h : h + 1] * s for f, s in zip(all_f, states)).astype(BF)
        before[r, :] = sum(f[:, h : h + 1] * s for f, s in zip(before_f, states))
    total[512:528, :] = log_row(sum(logs))
    passed = sum(jnp.where(place < pos, log, 0.0) for place, log in zip(places, logs))
    before[512:528, :] = jnp.concatenate([passed, jnp.zeros_like(passed)], axis=1)


def last_kernel(sc, p0, p1, p2, p3, before, mine, got, keep, give):
    pos, front = sc[0], sc[1] == 0
    pieces = (p0, p1, p2, p3)
    places = [(pos - d + 4) % 4 for d in range(4)]
    logs = [read_logs(p) for p in pieces]
    factors = []
    for place in places:
        late = jnp.zeros_like(logs[0])
        for other, log in zip(places, logs):
            late = late + jnp.where((other > place) & (other < pos), log, 0.0)
        factors.append(jnp.transpose(jnp.where(place < pos, jnp.exp(late), 0.0)))
    passed = jnp.transpose(jnp.exp(before[512:528, 0:128]))
    own = jnp.transpose(jnp.exp(jnp.where(front, read_logs(mine), read_logs(got))))
    for h in range(4):
        r = slice(128 * h, 128 * h + 128)
        col = slice(h, h + 1)
        far = sum(f[:, col] * p[r, :].astype(F32) for f, p in zip(factors[1:], pieces[1:]))
        enter = passed[:, col] * far + before[r, :]
        first = jnp.where(front, mine[r, :].astype(F32), got[r, :].astype(F32))
        second = own[:, col] * enter + first
        keep[r, :] = jnp.where(front, enter, second).astype(BF)
        give[r, :] = jnp.where(front, second, enter).astype(BF)


def small_call(kernel, name, scalars, arrays, outs):
    return pl.pallas_call(
        kernel,
        grid_spec=pltpu.PrefetchScalarGridSpec(
            num_scalar_prefetch=1,
            grid=(1,),
            in_specs=[pl.BlockSpec(a.shape, lambda i, s: (0, 0)) for a in arrays],
            out_specs=[pl.BlockSpec(o.shape, lambda i, s: (0, 0)) for o in outs],
        ),
        out_shape=outs,
        compiler_params=params(),
        name=name,
    )(jnp.stack(scalars), *arrays)


def enter_states(packed, place, back):
    c, x, z = place
    order = [1 - c, 3 - x, 3 - z] if back else [c, x, z]
    sign = -1 if back else 1
    out = lambda rows, dtype: jax.ShapeDtypeStruct((rows, 256), dtype)
    mine, got = pick(packed, c), shift(pick(packed, 1 - c), "c")
    (chip,) = small_call(core_kernel, "core_states", [order[0]], [mine, got], [out(528, BF)])
    parts = [chip] + [shift(chip, "x", sign * d) for d in (1, 2, 3)]
    total, before = small_call(
        axis_kernel, "axis_states", [order[1]], parts, [out(528, BF), out(528, F32)]
    )
    parts = [total] + [shift(total, "z", sign * d) for d in (1, 2, 3)]
    keep, give = small_call(
        last_kernel,
        "last_states",
        [order[2], order[0]],
        parts + [before, mine, got],
        [out(512, BF), out(512, BF)],
    )
    return keep, shift(give, "c")


def mix_kernel(
    sc, qkv, within, oi, og, keep, recv, hg, wout, x, fgain, mixed, branch, middle, second, acc
):
    j = pl.program_id(0)
    c = sc[1]
    for b in range(2):
        r = slice(128 * b, 128 * b + 128)
        q = qkv[r, 0:128].astype(F32) * QS
        qabs = (q * jnp.exp(within[r, :])).astype(BF)
        state = jnp.where(c == b, keep[...].astype(F32), recv[...].astype(F32)).astype(BF)
        mixed[r, :] = oi[r, :] + dot_nn(qabs, state)
    m = mixed[...]
    unit = m * lax.rsqrt(jnp.mean(m * m, axis=-1, keepdims=True) + EPS)
    g = og[...]
    part = (unit * hg[...] * (g * jax.nn.sigmoid(g))).astype(BF)
    branch[...] = part
    more = dot_nn(part, wout[...])

    @pl.when(j == 0)
    def _():
        acc[...] = x[...].astype(F32) + more

    @pl.when(j > 0)
    def _():
        acc[...] = acc[...] + more

    @pl.when(j == 3)
    def _():
        mid = acc[...]
        middle[...] = mid
        scale = lax.rsqrt(jnp.mean(mid * mid, axis=-1, keepdims=True) + EPS)
        second[...] = (mid * scale * fgain[...]).astype(BF)


def head_specs():
    def head(rows, width):
        return pl.BlockSpec((rows, width), lambda j, s: (0, (s[0] + j) % 4))

    def rel(width):
        return pl.BlockSpec((256, width), lambda j, s: (0, j))

    def whole(shape):
        return pl.BlockSpec(shape, lambda j, s: (0,) * len(shape))

    def state():
        return pl.BlockSpec((128, 256), lambda j, s: ((s[0] + j) % 4, 0))

    return head, rel, whole, state


def mix_rows(sc, qkv, within, oi, og, keep, recv, hg, wout, x, fgain):
    head, rel, whole, state = head_specs()
    out = lambda dtype: jax.ShapeDtypeStruct((256, 1024), dtype)
    return pl.pallas_call(
        mix_kernel,
        grid_spec=pltpu.PrefetchScalarGridSpec(
            num_scalar_prefetch=1,
            grid=(4,),
            in_specs=[
                head(256, 512),
                head(256, 128),
                head(256, 256),
                head(256, 256),
                state(),
                state(),
                whole((1, 256)),
                pl.BlockSpec((256, 1024), lambda j, s: (j, 0)),
                whole((256, 1024)),
                whole((1, 1024)),
            ],
            out_specs=[head(256, 256), rel(256), whole((256, 1024)), whole((256, 1024))],
            scratch_shapes=[pltpu.VMEM((256, 1024), F32)],
        ),
        out_shape=[out(F32), out(BF), out(F32), out(BF)],
        compiler_params=params(),
        name="mix_rows",
    )(sc, qkv, within, oi, og, keep, recv, hg, wout, x, fgain)


def ffn_kernel(second, dh, wg, wu, hidden, dg, du, ds, acc):
    i = pl.program_id(0)
    rows = second[...]
    gate = dot_nn(rows, wg[...])
    up = dot_nn(rows, wu[...])
    s = jax.nn.sigmoid(gate)
    silu = gate * s
    hidden[...] = (silu * up).astype(BF)
    d = dh[...].astype(F32)
    dgate = (d * up * s * (1.0 + gate * (1.0 - s))).astype(BF)
    dup = (d * silu).astype(BF)
    dg[...] = dgate
    du[...] = dup
    more = dot_nt(dgate, wg[...]) + dot_nt(dup, wu[...])

    @pl.when(i == 0)
    def _():
        acc[...] = more

    @pl.when(i > 0)
    def _():
        acc[...] = acc[...] + more

    @pl.when(i == 2)
    def _():
        ds[...] = acc[...].astype(BF)


def ffn_rows(second, dh, wgu):
    whole = pl.BlockSpec((256, 1024), lambda i: (0, 0))
    part = pl.BlockSpec((256, 256), lambda i: (0, i))
    out = lambda width: jax.ShapeDtypeStruct((256, width), BF)
    return pl.pallas_call(
        ffn_kernel,
        grid=(3,),
        in_specs=[
            whole,
            part,
            pl.BlockSpec((1024, 256), lambda i: (0, i)),
            pl.BlockSpec((1024, 256), lambda i: (0, 3 + i)),
        ],
        out_specs=[part, part, part, whole],
        scratch_shapes=[pltpu.VMEM((256, 1024), F32)],
        out_shape=[out(FFP), out(FFP), out(FFP), out(1024)],
        compiler_params=params(),
        name="ffn_rows",
    )(second, dh, wgu, wgu)


def down_kernel(
    sc, s0, s1, s2, s3, middle, fgain, grad, wout, mixed, og, hg, qkv, within, logs,
    dmiddle, dbo, gffn, ghead, dog, dmix, dpk,
):
    j = pl.program_id(0)
    h = (sc[0] + j) % 4

    @pl.when(j == 0)
    def _():
        ds = s0[...].astype(F32) + s1[...].astype(F32) + s2[...].astype(F32) + s3[...].astype(F32)
        mid = middle[...]
        scale = lax.rsqrt(jnp.mean(mid * mid, axis=-1, keepdims=True) + EPS)
        unit = mid * scale
        gffn[...] = jnp.sum(ds * unit, axis=0, keepdims=True)
        e = ds * fgain[...]
        dm = grad[...].astype(F32) + scale * (e - unit * jnp.mean(e * unit, axis=-1, keepdims=True))
        dmiddle[...] = dm
        dbo[...] = dm.astype(BF)
        ghead[...] = jnp.zeros_like(ghead)
        dpk[:, 512:528, :] = logs[...]

    db = dot_nt(dbo[...], wout[...]).astype(BF).astype(F32)
    m = mixed[...]
    scale = lax.rsqrt(jnp.mean(m * m, axis=-1, keepdims=True) + EPS)
    unit = m * scale
    g = og[...]
    s = jax.nn.sigmoid(g)
    swish = g * s
    ghead[...] += jnp.sum(db * unit * swish, axis=0, keepdims=True)
    gain = hg[...]
    dog[...] = (db * unit * gain * (s + g * s * (1.0 - s))).astype(BF)
    e = db * gain * swish
    dm = (scale * (e - unit * jnp.mean(e * unit, axis=-1, keepdims=True))).astype(BF)
    dmix[...] = dm
    for b in range(2):
        r = slice(128 * b, 128 * b + 128)
        q = qkv[r, 0:128].astype(F32) * QS
        qabs = (q * jnp.exp(within[r, :])).astype(BF)
        dpk[b, pl.ds(pl.multiple_of(h * 128, 128), 128), :] = dot_tn(qabs, dm[r]).astype(BF)


def down_rows(sc, parts, middle, fgain, grad, wout, mixed, og, hg, qkv, within, spk):
    head, rel, whole, state = head_specs()
    out = lambda shape, dtype: jax.ShapeDtypeStruct(shape, dtype)
    full = whole((256, 1024))
    return pl.pallas_call(
        down_kernel,
        grid_spec=pltpu.PrefetchScalarGridSpec(
            num_scalar_prefetch=1,
            grid=(4,),
            in_specs=[full] * 5
            + [
                whole((1, 1024)),
                full,
                pl.BlockSpec((256, 1024), lambda j, s: (j, 0)),
                head(256, 256),
                head(256, 256),
                whole((1, 256)),
                head(256, 512),
                head(256, 128),
                pl.BlockSpec((2, 16, 256), lambda j, s: (0, 32, 0)),
            ],
            out_specs=[
                full,
                full,
                whole((1, 1024)),
                whole((1, 256)),
                head(256, 256),
                head(256, 256),
                whole((2, 528, 256)),
            ],
        ),
        out_shape=[
            out((256, 1024), F32),
            out((256, 1024), BF),
            out((1, 1024), F32),
            out((1, 256), F32),
            out((256, 1024), BF),
            out((256, 1024), BF),
            out((2, 528, 256), BF),
        ],
        compiler_params=params(),
        name="down_rows",
    )(sc, *parts, middle, fgain, grad, wout, mixed, og, hg, qkv, within, spk)


def back_kernel(
    sc, qkv, within, logits, dmix, keep, recv, dkeep, drecv, rank, wro,
    dcat, gro, gbias, drank,
):
    h = pl.program_id(0)
    c = sc[1]
    mask = causal_mask()
    upper = jnp.transpose(mask.astype(F32))
    left = pl.multiple_of(h * 512, 512)
    grads = []
    for b in range(2):
        r = slice(128 * b, 128 * b + 128)
        rows = qkv[r, :]
        q = rows[:, 0:128].astype(F32) * QS
        k = rows[:, 128:256].astype(F32)
        v = rows[:, 256:512]
        w = within[r, :]
        mid, tot = w[63:64], w[127:128]
        eq, ek, ew, ee = jnp.exp(w - mid), jnp.exp(mid - w), jnp.exp(w), jnp.exp(tot - w)
        qm, km = (q * eq).astype(BF), (k * ek).astype(BF)
        kend = k * ee
        do = dmix[r, :]
        scores = jnp.where(mask, dot_nt(qm, km), 0.0).astype(BF)
        dscores = jnp.where(mask, dot_nt(do, v), 0.0).astype(BF)
        state = jnp.where(c == b, keep[...].astype(F32), recv[...].astype(F32))
        dstate = jnp.where(c == b, dkeep[...].astype(F32), drecv[...].astype(F32))
        state_b, dstate_b = state.astype(BF), dstate.astype(BF)
        dqm, dkm = dot_nn(dscores, km), dot_tn(dscores, qm)
        dqi, dke = dot_nt(do, state_b), dot_nt(v, dstate_b)
        dv = dot_tn(scores, do) + dot_nn(kend.astype(BF), dstate_b)
        dq = (dqm * eq + dqi * ew) * QS
        dk = dkm * ek + dke * ee
        ends = kend * dke
        dw = qm.astype(F32) * dqm - km.astype(F32) * dkm + q * ew * dqi - ends
        cross = dot_nt(jnp.ones((8, 256), F32), state * dstate, HIGH)[0:1]
        dtot = jnp.sum(ends, axis=0, keepdims=True) + jnp.exp(tot) * cross
        dd = dot_nn(upper, dw, HIGH) + dtot
        dl = (dd * jax.nn.sigmoid(-logits[r, :]) / DECAY_NORM).astype(BF)
        grads.append(dl)
        dcat[r, pl.ds(left, 512)] = jnp.concatenate([dq, dk, dv], axis=1).astype(BF)
    dl = jnp.concatenate(grads, axis=0)
    gro[...] = dot_tn(rank[...], dl)[0:16]
    gbias[...] = jnp.sum(dl.astype(F32), axis=0, keepdims=True)
    more = dot_nt(dl, wro[...])

    @pl.when(h == 0)
    def _():
        drank[...] = more

    @pl.when(h > 0)
    def _():
        drank[...] = drank[...] + more

    @pl.when(h == 3)
    def _():
        dcat[:, 2048:2176] = drank[...].astype(BF)


def back_rows(sc, qkv, within, logits, dmix, keep, recv, dkeep, drecv, rank, wro):
    def cols(rows, width):
        return pl.BlockSpec((rows, width), lambda h, s: (0, h))

    def whole(shape):
        return pl.BlockSpec(shape, lambda h, s: (0,) * len(shape))

    state = pl.BlockSpec((128, 256), lambda h, s: (h, 0))
    out = lambda shape, dtype: jax.ShapeDtypeStruct(shape, dtype)
    return pl.pallas_call(
        back_kernel,
        grid_spec=pltpu.PrefetchScalarGridSpec(
            num_scalar_prefetch=1,
            grid=(4,),
            in_specs=[
                cols(256, 512),
                cols(256, 128),
                cols(256, 128),
                cols(256, 256),
                state,
                state,
                state,
                state,
                whole((256, 128)),
                cols(128, 128),
            ],
            out_specs=[whole((256, 2176)), cols(16, 128), cols(1, 128)],
            scratch_shapes=[pltpu.VMEM((256, 128), F32)],
        ),
        out_shape=[out((256, 2176), BF), out((16, 512), F32), out((1, 512), F32)],
        compiler_params=params(),
        name="back_rows",
    )(sc, qkv, within, logits, dmix, keep, recv, dkeep, drecv, rank, wro)


def input_kernel(sc, dcat, dog, wqr, wog, x, gain, dmiddle, grad, gnorm, acc):
    j = pl.program_id(0)
    y = sc[0]
    acc[j] = dot_nt(dcat[...], wqr[...]) + dot_nt(dog[...], wog[...])

    @pl.when(j == 3)
    def _():
        xf = x[...].astype(F32)
        scale = lax.rsqrt(jnp.mean(xf * xf, axis=-1, keepdims=True) + EPS)
        units, es = [], []
        total = jnp.zeros((256, 1), F32)
        for i in range(4):
            at = pl.multiple_of(((y + i) % 4) * 256, 256)
            unit = x[:, pl.ds(at, 256)].astype(F32) * scale
            d = acc[i]
            cols = slice(i * 256, i * 256 + 256)
            gnorm[:, cols] = jnp.sum(d * unit, axis=0, keepdims=True)
            e = d * gain[:, cols]
            total = total + jnp.sum(e * unit, axis=-1, keepdims=True)
            units.append(unit)
            es.append(e)
        mean = total / 1024.0
        for i in range(4):
            at = pl.multiple_of(((y + i) % 4) * 256, 256)
            grad[:, pl.ds(at, 256)] = dmiddle[:, pl.ds(at, 256)] + scale * (
                es[i] - units[i] * mean
            )


def input_rows(sc, dcat, dog, wqr, wog, x, gain, dmiddle):
    def whole(shape):
        return pl.BlockSpec(shape, lambda j, s: (0,) * len(shape))

    full = whole((256, 1024))
    return pl.pallas_call(
        input_kernel,
        grid_spec=pltpu.PrefetchScalarGridSpec(
            num_scalar_prefetch=1,
            grid=(4,),
            in_specs=[
                whole((256, 2176)),
                full,
                pl.BlockSpec((256, 2176), lambda j, s: (j, 0)),
                pl.BlockSpec((256, 1024), lambda j, s: (j, 0)),
                full,
                whole((1, 1024)),
                full,
            ],
            out_specs=[full, whole((1, 1024))],
            scratch_shapes=[pltpu.VMEM((4, 256, 256), F32)],
        ),
        out_shape=[
            jax.ShapeDtypeStruct((256, 1024), F32),
            jax.ShapeDtypeStruct((1, 1024), F32),
        ],
        compiler_params=params(),
        name="input_rows",
    )(sc, dcat, dog, wqr, wog, x, gain, dmiddle)


def plane_sum(rows, first, second, place, extra=None):
    tail = [] if extra is None else [extra]

    def step(value, count, axis):
        me = place[axis]

        def block(d):
            start = ((me + d) % 4) * count
            part = lax.dynamic_slice_in_dim(value, start, count, axis=0)
            return jnp.concatenate([part, value[4 * count :]], axis=0) if tail else part

        return spread(block, axis).astype(BF)

    value = jnp.concatenate([rows] + tail, axis=0) if tail else rows
    value = step(value, 32, first)
    return step(value, 8, second)


def plane_all(rows, first, second, place):
    part = in_order(fetch(rows, second), place[second])
    return in_order(fetch(part, first), place[first])


def core_all(rows, core):
    other = shift(rows, "c")
    return jnp.where(
        core == 0,
        jnp.concatenate([rows, other], axis=0),
        jnp.concatenate([other, rows], axis=0),
    )


def shards(
    inputs, lengths, norm_gain, w_query, w_key, w_value, w_outgate, w_rank_in, w_rank_out,
    rank_bias, head_gain, w_output, ffn_gain, w_gate, w_up, w_down, cotangent,
):
    y, s = lax.axis_index("wsh"), lax.axis_index("seq")
    c, x, z = s % 2, (s // 2) % 4, s // 8
    place = {"c": c, "x": x, "z": z, "y": y}
    sc = jnp.stack([y, c])
    rows_in = inputs.reshape(256, 1024)

    packed = []
    for h in range(H):
        packed += [
            w_query[:, h * HK : h * HK + HK],
            w_key[:, h * HK : h * HK + HK],
            w_value[:, h * HV : h * HV + HV],
        ]
    packed = jnp.concatenate(packed + [w_outgate, jnp.pad(w_rank_in, ((0, 0), (0, 112)))], axis=1)
    small = jnp.concatenate([norm_gain, ffn_gain, head_gain, rank_bias, w_rank_out.reshape(2048)])
    small = jnp.pad(small[None], ((0, 15), (0, 448)))
    half = lax.dynamic_slice_in_dim(packed, c * 128, 128, axis=0)
    mine = fetch(jnp.concatenate([half, small], axis=0), "y")[1:]
    got = [shift(m, "c") for m in mine]
    smalls_rel = jnp.concatenate([small[0:1]] + [m[128:129] for m in mine], axis=0)
    smalls = in_order([smalls_rel[d : d + 1] for d in range(4)], y).astype(F32)
    gain_rel = smalls_rel[:, 0:256].astype(F32).reshape(1, 1024)
    fgain = smalls[:, 256:512].reshape(1, 1024)
    hgain = smalls[:, 512:576].reshape(1, 256)
    bias = smalls[:, 576:704].reshape(1, 512)
    wro = jnp.pad(smalls[:, 704:2752].reshape(16, 512).astype(BF), ((0, 112), (0, 0)))

    normed, wqr, wog, qkv, og, rank, logits, within, oi, spk = project_rows(
        sc, rows_in, gain_rel, wro, bias, packed, mine, got
    )

    half = lax.dynamic_slice_in_dim(w_output, c * 128, 128, axis=0)
    half = after(half, *got)
    wout_mine = fetch(half, "y")[1:]
    wout = [w_output] + [core_all(m, c) for m in wout_mine]
    wout = jnp.concatenate(wout, axis=0)

    gap = jnp.zeros((256, FFP - 704), BF)
    blocks = []
    for j in range(4):
        cols = slice(704 * j, 704 * j + 704)
        blocks.append(jnp.concatenate([w_gate[:, cols], gap, w_up[:, cols], gap], axis=1))
    blocks = jnp.stack(blocks)
    half = lax.dynamic_slice_in_dim(blocks, c * 128, 128, axis=1)
    half = after(half, *got)
    wgu = {d: shift(pick(half, (y + d) % 4), "y", d) for d in (2, 1, 3)}
    wgu = [pick(blocks, y)] + [core_all(wgu[d], c) for d in (3, 2, 1)]
    wgu = in_order(wgu, y)

    positions = s * 128 + jnp.arange(128, dtype=jnp.int32)
    valid = positions[None, :] < lengths[:, None]
    grad = jnp.where(valid[..., None], cotangent, jnp.zeros_like(cotangent)).reshape(256, 1024)
    grad_all = jnp.concatenate(fetch(after(grad, *got), "y"), axis=0)
    wdown = jnp.pad(w_down, ((0, FFP - 704), (0, 0)))
    d_hidden = dot_nt(grad_all, wdown).astype(BF)

    keep, recv = enter_states(spk, (c, x, z), False)
    mixed, branch, middle, second = mix_rows(
        sc, qkv, within, oi, og, keep, recv, hgain, wout, rows_in, fgain
    )

    seconds = fetch(second, "y")
    hidden, dgu, parts = [], [], {}
    for d in range(4):
        hid, dg, du, ds = ffn_rows(seconds[d], d_hidden[256 * d : 256 * d + 256], wgu)
        hidden.append(hid)
        dgu.append(jnp.concatenate([dg, du], axis=1))
        parts[d] = ds if d == 0 else shift(ds, "y", d)

    dmiddle, dbo, gffn, ghead, dog, dmix, dpk = down_rows(
        sc, [parts[d] for d in range(4)], middle, fgain, grad, wout, mixed, og, hgain, qkv, within,
        spk,
    )
    dkeep, drecv = enter_states(dpk, (c, x, z), True)

    def part_out(d):
        return dot_nn(hidden[d], wdown).astype(BF)

    outputs = middle + spread(part_out, "y")

    hidden_all = jnp.concatenate(hidden, axis=0)
    second_all = jnp.concatenate(seconds, axis=0)
    dgu_all = jnp.concatenate(dgu, axis=0)
    g_gu = dot_tn(second_all, dgu_all).astype(BF).reshape(4, 2, 128, 2 * FFP)
    g_down = dot_tn(hidden_all, grad_all)[:704].astype(BF)
    g_down = g_down.reshape(2, 11, 32, 4, 256).transpose(0, 3, 2, 1, 4).reshape(2, 128, 2816)
    g_oo = jnp.concatenate([dot_tn(normed, dog), dot_tn(branch, dbo)], axis=1).astype(BF)
    g_oo = g_oo.reshape(4, 2, 128, 2048)

    def core_sum(value, axis):
        return (
            pick(value, c, axis).astype(F32) + shift(pick(value, 1 - c, axis), "c").astype(F32)
        ).astype(BF)

    g_gu = core_sum(g_gu, 1)
    g_down = core_sum(g_down, 0)
    g_oo = core_sum(g_oo, 1)
    sent = {d: shift(pick(g_gu, (y + d) % 4), "y", d) for d in (2, 1, 3)}
    g_gu = [pick(g_gu, y), sent[1], sent[2], sent[3]]
    g_oo = spread(lambda d: g_oo[d], "y").astype(BF)
    early = jnp.concatenate(g_gu + [g_oo, g_down], axis=1)
    early_a = plane_sum(early[:, :5504], "x", "z", place)
    early_b = plane_sum(early[:, 5504:], "z", "x", place)

    dcat, gro, gbias = back_rows(
        sc, qkv, within, logits, dmix, keep, recv, dkeep, drecv, rank, wro
    )
    input_grad, gnorm = input_rows(sc, dcat, dog, wqr, wog, rows_in, gain_rel, dmiddle)

    late = dot_tn(normed, dcat).astype(BF).reshape(4, 2, 128, 2176)
    line0 = jnp.pad(gro.reshape(4, 1, 2048), ((0, 0), (0, 0), (0, 128)))
    line1 = jnp.concatenate(
        [gffn.reshape(4, 256), ghead.reshape(4, 64), gbias.reshape(4, 128)], axis=1
    )
    line1 = jnp.pad(line1, ((0, 0), (0, 2176 - 448)))[:, None]
    extra = from_me(jnp.concatenate([line0, line1], axis=1), y)
    line2 = jnp.pad(gnorm.reshape(4, 1, 256), ((0, 0), (0, 0), (0, 1920)))
    extra = jnp.concatenate([extra, line2], axis=1).astype(BF)
    extra = jnp.pad(extra, ((0, 0), (0, 13), (0, 0)))
    late_own = jnp.concatenate([pick(late, c, 1), extra], axis=1)
    late_far = jnp.concatenate([pick(late, 1 - c, 1), extra], axis=1)
    late = (late_own.astype(F32) + shift(late_far, "c").astype(F32)).astype(BF)
    late = spread(lambda d: late[d], "y").astype(BF)
    late = plane_sum(late[:128], "x", "z", place, late[128:])
    ends = late[8:].astype(F32)
    late = core_all(plane_all(late[:8], "x", "z", place), c)

    early_a = core_all(plane_all(early_a, "x", "z", place), c)
    early_b = core_all(plane_all(early_b, "z", "x", place), c)
    early = jnp.concatenate([early_a, early_b], axis=1)
    g_gu = [early[:, 2 * FFP * i : 2 * FFP * (i + 1)] for i in range(4)]
    g_gu = in_order([g[None] for g in (g_gu[0], g_gu[3], g_gu[2], g_gu[1])], y)
    grad_gate = jnp.concatenate([g_gu[j, :, :704] for j in range(4)], axis=1).astype(F32)
    grad_up = jnp.concatenate([g_gu[j, :, FFP : FFP + 704] for j in range(4)], axis=1).astype(F32)
    grad_outgate = early[:, 6144:7168].astype(F32)
    grad_output = early[:, 7168:8192].astype(F32)
    g_down = early[:, 8192:].reshape(2, 4, 32, 11, 256).transpose(0, 3, 2, 1, 4)
    grad_down = g_down.reshape(704, 1024).astype(F32)

    def heads(start, width):
        cols = [late[:, 512 * h + start : 512 * h + start + width] for h in range(H)]
        return jnp.concatenate(cols, axis=1).astype(F32)

    return (
        outputs.reshape(inputs.shape),
        input_grad.reshape(inputs.shape),
        ends[2, :256],
        heads(0, 128),
        heads(128, 128),
        heads(256, 256),
        grad_outgate,
        late[:, 2048:2064].astype(F32),
        ends[0, :2048].reshape(4, 512),
        ends[1, 320:448],
        ends[1, 256:320],
        grad_output,
        ends[1, :256],
        grad_gate,
        grad_up,
        grad_down,
    )


def solution(mesh):
    rows, vector, matrix = P("wsh", "seq", None), P("wsh"), P("wsh", None)
    placed = (
        rows, vector, vector, matrix, matrix, matrix, matrix, matrix, matrix, vector, vector,
        matrix, vector, matrix, matrix, matrix, rows,
    )
    return jax.shard_map(
        shards,
        mesh=mesh,
        in_specs=placed,
        out_specs=(
            rows, rows, vector, matrix, matrix, matrix, matrix, matrix, matrix, vector, vector,
            matrix, vector, matrix, matrix, matrix,
        ),
        check_vma=False,
    )
```
